32 devices in a mesh: row: 8 (over y, x, core), col: 4 (over z).
Axes of the slice: x: 2, y: 2, z: 4, core: 2. Of those that a mesh axis runs over, the one named last changes fastest.
Arguments:
- matrix: float32 [61440, 1536], P('row', 'col'), may hold values from -1 to 96, as said below
Outputs:
- stepped: float32 [61440, 1536], P('row', 'col')
The draws below stay inside these ranges and needn't reach their ends.
Inputs may be any that keep to these rules, and one draw needn't show every extreme that they name: `matrix`: entries where global row equals global column lie in 64 to 96; all other entries lie in -1 to 1, so the symmetrized first diagonal tile is positive definite.
All inputs are finite; a program needn't handle non-finite values.
Results may differ from the reference program's by a relative error of at most 0.0003.
Values sent between devices are 32-bit elements; how exact they have to be, the bound alone decides.
A program may use at most 64 MiB of HBM per device.

```python
import jax
import jax.numpy as jnp
from jax import lax

N = 61440
B = 64
PROWS = 8
PCOLS = 4
W = 1536


def draw_matrix(key, part):
    rows_dev = N // PROWS
    cols_dev = W // PCOLS
    srow = jnp.arange(N, dtype=jnp.int32)
    local = srow % rows_dev
    global_rows = (local // B * PROWS + srow // rows_dev) * B + local % B
    scol = jnp.arange(W, dtype=jnp.int32)
    clocal = scol % cols_dev
    global_cols = (clocal // B * PCOLS + scol // cols_dev) * B + clocal % B
    key_off = jax.random.fold_in(key, 11)
    key_diag = jax.random.fold_in(key, 23)
    offdiag = jax.random.uniform(key_off, (N, W), jnp.float32, -1.0, 1.0)
    diagonal = jax.random.uniform(key_diag, (N, W), jnp.float32, 64.0, 96.0)
    same = global_rows[:, None] == global_cols[None, :]
    return jnp.where(same, diagonal, offdiag)


def setup_inputs(seed: int = 0) -> dict:
    streams_of = jax.random.split(jax.random.key(seed), 2)
    matrix = draw_matrix(jax.random.fold_in(streams_of[1], 71), 0)
    return {"matrix": matrix}


def reference(matrix):
    rows_dev = N // PROWS
    cols_dev = W // PCOLS
    srow = jnp.arange(N, dtype=jnp.int32)
    owner = srow // rows_dev
    local = srow % rows_dev
    global_rows = (local // B * PROWS + owner) * B + local % B
    scol = jnp.arange(W, dtype=jnp.int32)
    cowner = scol // cols_dev
    clocal = scol % cols_dev
    global_cols = (clocal // B * PCOLS + cowner) * B + clocal % B
    tile = matrix[:B, :B]
    corner = (tile + tile.T) / 2.0
    factor = jnp.linalg.cholesky(corner)
    solved = lax.linalg.triangular_solve(factor, matrix[:, :B].T, left_side=True, lower=True)
    panel_factor = solved.T
    panel_factor = panel_factor.at[:B].set(factor)
    tiles = global_cols // B
    where_row = tiles % PROWS * rows_dev + tiles // PROWS * B + global_cols % B
    column_factor = jnp.take(panel_factor, where_row.astype(jnp.int32), axis=0)
    blocks = matrix.reshape(PROWS, rows_dev, W)
    lower_blocks = panel_factor.reshape(PROWS, rows_dev, B)
    grow_blocks = global_rows.reshape(PROWS, rows_dev)

    def update_block(items):
        block, lower, grow = items
        change = jnp.dot(lower.astype(jnp.float32), column_factor.T.astype(jnp.float32), precision=lax.Precision.HIGHEST, preferred_element_type=jnp.float32)
        return jnp.where((grow < B)[:, None], block, block - change)
    stepped = lax.map(update_block, (blocks, lower_blocks, grow_blocks)).reshape(N, W)
    stepped = stepped.at[:, :B].set(panel_factor)
    return stepped
```

```python
import functools

import jax
import jax.numpy as jnp
from jax import lax
from jax.experimental import pallas as pl
from jax.experimental.pallas import tpu as pltpu
from jax.sharding import PartitionSpec as P

B = 64
R = 256
H = R // 2
LANES = 128
GROUP = 8
LEAD = 3
MESH = pl.DeviceIdType.MESH
HI = lax.Precision.HIGHEST


def mm(a, b, contract):
    return lax.dot_general(
        a, b, ((contract[:1], contract[1:]), ((), ())), precision=HI, preferred_element_type=jnp.float32
    )


def kernel(n_row, n_col, a_ref, a_v, pack, corner_b, cols_b, m_b, head,
           a_in, f_send, f_recv, k_send, k_recv, c_send, c_recv):
    p = lax.axis_index("row")
    q = lax.axis_index("col")
    rows, width = a_v.shape
    n = rows // R
    per = n_row // n_col
    last = n_col - 1

    def fetch(c):
        at = pl.ds(pl.multiple_of(c * R, R), R)
        return pltpu.make_async_copy(a_ref.at[at], a_v.at[at], a_in.at[c])

    def hop(c):
        at = pl.ds(pl.multiple_of(c * H, H), H)
        return pltpu.make_async_remote_copy(
            src_ref=pack.at[at], dst_ref=pack.at[at], send_sem=f_send.at[c], recv_sem=f_recv.at[c],
            device_id=(p, lax.rem(q + 1, n_col)), device_id_type=MESH,
        )

    def peer(i):
        return lax.rem(p + i, n_row), q

    def send_corner(i):
        return pltpu.make_async_remote_copy(
            src_ref=pack.at[pl.ds(0, B)], dst_ref=corner_b, send_sem=k_send.at[i - 1], recv_sem=k_recv.at[0],
            device_id=peer(i), device_id_type=MESH,
        )

    def send_cols(i, slot):
        return pltpu.make_async_remote_copy(
            src_ref=pack.at[pl.ds(0, H)], dst_ref=cols_b.at[slot], send_sem=c_send.at[i - 1],
            recv_sem=c_recv.at[slot], device_id=peer(i), device_id_type=MESH,
        )

    for c in range(n):
        fetch(c).start()

    barrier = pltpu.get_barrier_semaphore()
    for i in range(1, n_row):
        pl.semaphore_signal(barrier, inc=1, device_id=peer(i), device_id_type=MESH)

    @pl.when(q > 0)
    def _():
        pl.semaphore_signal(barrier, inc=1, device_id=(p, q - 1), device_id_type=MESH)

    @pl.when(q < last)
    def _():
        pl.semaphore_signal(barrier, inc=1, device_id=(p, q + 1), device_id_type=MESH)

    ends = jnp.where(q > 0, 1, 0) + jnp.where(q < last, 1, 0)
    pl.semaphore_wait(barrier, n_row - 1 + ends)

    lane = lax.broadcasted_iota(jnp.int32, (H, LANES), 1)

    def source(c):
        fetch(c).wait()
        base = pl.multiple_of(c * R, R)
        top = a_v[pl.ds(base, H), :LANES]
        low = a_v[pl.ds(base + H, H), :LANES]
        pack[pl.ds(pl.multiple_of(c * H, H), H), :] = jnp.where(lane < B, top, pltpu.roll(low, B, 1))
        hop(c).start()

    def forward(c):
        @pl.when(q > 0)
        def _():
            fetch(c).wait()
            hop(c).wait_recv()

            @pl.when(q < last)
            def _():
                hop(c).start()

    @pl.when(q == 0)
    def _():
        source(0)

    forward(0)
    head[...] = a_v[:B, :]
    mine = p // n_col
    owner = lax.rem(p, n_col) == q

    @pl.when(p == 0)
    def _():
        for i in range(1, n_row):
            send_corner(i).start()
        corner_b[...] = pack[:B, :]

    @pl.when(owner)
    def _():
        for i in range(1, n_row):
            send_cols(i, mine).start()
        cols_b[mine] = pack[:H, :]

    @pl.when(q == 0)
    def _():
        @pl.loop(1, n)
        def _(c):
            source(c)

    done = 1
    while done < min(1 + LEAD, n):
        forward(done)
        done += 1

    @pl.when(p != 0)
    def _():
        send_corner(1).wait_recv()

    raw = corner_b[...][:, :B]
    corner = (raw + raw.T) / 2.0
    row64 = lax.broadcasted_iota(jnp.int32, (B, B), 0)
    col64 = lax.broadcasted_iota(jnp.int32, (B, B), 1)
    eye = jnp.where(row64 == col64, 1.0, 0.0)
    aug = jnp.concatenate([corner, eye], axis=1)
    row_id = lax.broadcasted_iota(jnp.int32, (B, 1), 0)
    for k in range(B):
        scale = 1.0 / aug[k:k + 1, k:k + 1]
        weight = jnp.where(row_id > k, aug[:, k:k + 1] * scale, 0.0)
        aug = aug - weight * aug[k:k + 1, :]
        if k % GROUP == GROUP - 1 and done < n:
            forward(done)
            done += 1
    pivots = jnp.sum(jnp.where(row64 == col64, aug[:, :B], 0.0), axis=1, keepdims=True)
    inv = pltpu.roll(aug, B, 1)[:, :B] / jnp.sqrt(pivots)
    inv_t = inv.T
    sinv = mm(inv_t, inv, (1, 0))

    for slot in range(per):
        @pl.when(p != q + slot * n_col)
        def _(slot=slot):
            send_cols(1, slot).wait_recv()

    tiles = []
    for j in range(width // B):
        at = j // per * B
        block = cols_b[j % per, at % H:at % H + B, :]
        if at >= H:
            block = pltpu.roll(block, B, 1)
        tiles.append(block[:, :B])
    m = mm(sinv, jnp.concatenate(tiles, axis=0), (1, 1))
    first = q == 0
    m_first = jnp.where(first, -inv_t, m[:, :B])
    m = jnp.concatenate([m_first, m[:, B:]], axis=1)
    m_b[...] = jnp.zeros_like(m_b)
    m_b[:B, :width] = m
    m_b[B:, width:] = m
    factor = jnp.where(row64 >= col64, mm(corner, inv_t, (1, 0)), 0.0)
    head[:, :B] = jnp.where(first, factor, head[:, :B])
    wide = lax.broadcasted_iota(jnp.int32, (H, width), 1)
    drop = jnp.logical_and(first, wide < B)

    def update(c):
        change = mm(pack[pl.ds(pl.multiple_of(c * H, H), H), :], m_b[...], (1, 0))
        base = pl.multiple_of(c * R, R)
        for half in range(2):
            at = pl.ds(base + half * H, H)
            a_v[at, :] = jnp.where(drop, 0.0, a_v[at, :]) - change[:, half * width:(half + 1) * width]

        @pl.when(jnp.logical_and(p == 0, c == 0))
        def _():
            a_v[:B, :] = head[...]

    paired = min(done, n - done)

    @pl.loop(0, paired)
    def _(i):
        forward(done + i)
        update(2 * i)
        update(2 * i + 1)

    @pl.loop(2 * paired, n)
    def _(c):
        @pl.when(c >= done + paired)
        def _():
            forward(c)

        update(c)

    @pl.when(q < last)
    def _():
        @pl.loop(0, n)
        def _(c):
            hop(c).wait_send()

    @pl.when(p == 0)
    def _():
        for i in range(1, n_row):
            send_corner(i).wait_send()

    @pl.when(owner)
    def _():
        for i in range(1, n_row):
            send_cols(i, mine).wait_send()


def solution(mesh):
    n_row, n_col = mesh.shape["row"], mesh.shape["col"]

    def step(matrix):
        rows, width = matrix.shape
        n = rows // R
        per = n_row // n_col
        assert rows % R == 0 and n_row % n_col == 0 and width // B // per * B <= R
        return pl.pallas_call(
            functools.partial(kernel, n_row, n_col),
            out_shape=jax.ShapeDtypeStruct((rows, width), jnp.float32),
            in_specs=[pl.BlockSpec(memory_space=pltpu.HBM)],
            out_specs=pl.BlockSpec(memory_space=pltpu.VMEM),
            scratch_shapes=[
                pltpu.VMEM((rows // 2, LANES), jnp.float32),
                pltpu.VMEM((B, LANES), jnp.float32),
                pltpu.VMEM((per, H, LANES), jnp.float32),
                pltpu.VMEM((LANES, 2 * width), jnp.float32),
                pltpu.VMEM((B, width), jnp.float32),
                pltpu.SemaphoreType.DMA((n,)),
                pltpu.SemaphoreType.DMA((n,)),
                pltpu.SemaphoreType.DMA((n,)),
                pltpu.SemaphoreType.DMA((n_row - 1,)),
                pltpu.SemaphoreType.DMA((1,)),
                pltpu.SemaphoreType.DMA((n_row - 1,)),
                pltpu.SemaphoreType.DMA((per,)),
            ],
            compiler_params=pltpu.CompilerParams(
                collective_id=0, has_side_effects=True, vmem_limit_bytes=24 * 1024 * 1024
            ),
        )(pltpu.with_memory_space_constraint(matrix, pltpu.HBM))

    return jax.shard_map(
        step, mesh=mesh, in_specs=(P("row", "col"),), out_specs=P("row", "col"), check_vma=False
    )
```

```python
import functools

import jax
import jax.numpy as jnp
from jax import lax
from jax.experimental import pallas as pl
from jax.experimental.pallas import tpu as pltpu
from jax.sharding import PartitionSpec as P

B = 64
R = 256
H = R // 2
LANES = 128
GROUP = 8
LEAD = 3
MESH = pl.DeviceIdType.MESH
HI = lax.Precision.HIGHEST


def mm(a, b, contract):
    return lax.dot_general(
        a, b, ((contract[:1], contract[1:]), ((), ())), precision=HI, preferred_element_type=jnp.float32
    )


def kernel(n_row, n_col, a_ref, a_v, pack, corner_b, cols_b, m_b, head,
           a_in, f_send, f_recv, k_send, k_recv, c_send, c_recv):
    p = lax.axis_index("row")
    q = lax.axis_index("col")
    rows, width = a_v.shape
    n = rows // R
    per = n_row // n_col
    last = n_col - 1

    def fetch(c):
        at = pl.ds(pl.multiple_of(c * R, R), R)
        return pltpu.make_async_copy(a_ref.at[at], a_v.at[at], a_in.at[c])

    def hop(c):
        at = pl.ds(pl.multiple_of(c * H, H), H)
        return pltpu.make_async_remote_copy(
            src_ref=pack.at[at], dst_ref=pack.at[at], send_sem=f_send.at[c], recv_sem=f_recv.at[c],
            device_id=(p, lax.rem(q + 1, n_col)), device_id_type=MESH,
        )

    def peer(i):
        return lax.rem(p + i, n_row), q

    def send_corner(i):
        return pltpu.make_async_remote_copy(
            src_ref=pack.at[pl.ds(0, B)], dst_ref=corner_b, send_sem=k_send.at[i - 1], recv_sem=k_recv.at[0],
            device_id=peer(i), device_id_type=MESH,
        )

    def send_cols(i, slot):
        return pltpu.make_async_remote_copy(
            src_ref=pack.at[pl.ds(0, H)], dst_ref=cols_b.at[slot], send_sem=c_send.at[i - 1],
            recv_sem=c_recv.at[slot], device_id=peer(i), device_id_type=MESH,
        )

    for c in range(n):
        fetch(c).start()

    barrier = pltpu.get_barrier_semaphore()
    for i in range(1, n_row):
        pl.semaphore_signal(barrier, inc=1, device_id=peer(i), device_id_type=MESH)

    @pl.when(q > 0)
    def _():
        pl.semaphore_signal(barrier, inc=1, device_id=(p, q - 1), device_id_type=MESH)

    @pl.when(q < last)
    def _():
        pl.semaphore_signal(barrier, inc=1, device_id=(p, q + 1), device_id_type=MESH)

    ends = jnp.where(q > 0, 1, 0) + jnp.where(q < last, 1, 0)
    pl.semaphore_wait(barrier, n_row - 1 + ends)

    lane = lax.broadcasted_iota(jnp.int32, (H, LANES), 1)

    def source(c):
        fetch(c).wait()
        base = pl.multiple_of(c * R, R)
        top = a_v[pl.ds(base, H), :LANES]
        low = a_v[pl.ds(base + H, H), :LANES]
        pack[pl.ds(pl.multiple_of(c * H, H), H), :] = jnp.where(lane < B, top, pltpu.roll(low, B, 1))
        hop(c).start()

    def forward(c):
        @pl.when(q > 0)
        def _():
            fetch(c).wait()
            hop(c).wait_recv()

            @pl.when(q < last)
            def _():
                hop(c).start()

    @pl.when(q == 0)
    def _():
        source(0)

    forward(0)
    head[...] = a_v[:B, :]
    mine = p // n_col
    owner = lax.rem(p, n_col) == q

    @pl.when(p == 0)
    def _():
        for i in range(1, n_row):
            send_corner(i).start()
        corner_b[...] = pack[:B, :]

    @pl.when(owner)
    def _():
        for i in range(1, n_row):
            send_cols(i, mine).start()
        cols_b[mine] = pack[:H, :]

    @pl.when(q == 0)
    def _():
        @pl.loop(1, n)
        def _(c):
            source(c)

    done = 1
    while done < min(1 + LEAD, n):
        forward(done)
        done += 1

    @pl.when(p != 0)
    def _():
        send_corner(1).wait_recv()

    raw = corner_b[...][:, :B]
    corner = (raw + raw.T) / 2.0
    row64 = lax.broadcasted_iota(jnp.int32, (B, B), 0)
    col64 = lax.broadcasted_iota(jnp.int32, (B, B), 1)
    eye = jnp.where(row64 == col64, 1.0, 0.0)
    aug = jnp.concatenate([corner, eye], axis=1)
    row_id = lax.broadcasted_iota(jnp.int32, (B, 1), 0)
    for k in range(B):
        scale = 1.0 / aug[k:k + 1, k:k + 1]
        weight = jnp.where(row_id > k, aug[:, k:k + 1] * scale, 0.0)
        aug = aug - weight * aug[k:k + 1, :]
        if k % GROUP == GROUP - 1 and done < n:
            forward(done)
            done += 1
    pivots = jnp.sum(jnp.where(row64 == col64, aug[:, :B], 0.0), axis=1, keepdims=True)
    inv = pltpu.roll(aug, B, 1)[:, :B] / jnp.sqrt(pivots)
    inv_t = inv.T
    sinv = mm(inv_t, inv, (1, 0))

    for slot in range(per):
        @pl.when(p != q + slot * n_col)
        def _(slot=slot):
            send_cols(1, slot).wait_recv()

    tiles = []
    for j in range(width // B):
        at = j // per * B
        block = cols_b[j % per, at % H:at % H + B, :]
        if at >= H:
            block = pltpu.roll(block, B, 1)
        tiles.append(block[:, :B])
    m = mm(sinv, jnp.concatenate(tiles, axis=0), (1, 1))
    first = q == 0
    m_first = jnp.where(first, -inv_t, m[:, :B])
    m = jnp.concatenate([m_first, m[:, B:]], axis=1)
    m_b[...] = jnp.zeros_like(m_b)
    m_b[:B, :width] = m
    m_b[B:, width:] = m
    factor = jnp.where(row64 >= col64, mm(corner, inv_t, (1, 0)), 0.0)
    head[:, :B] = jnp.where(first, factor, head[:, :B])
    wide = lax.broadcasted_iota(jnp.int32, (H, width), 1)
    drop = jnp.logical_and(first, wide < B)

    def update(c):
        change = mm(pack[pl.ds(pl.multiple_of(c * H, H), H), :], m_b[...], (1, 0))
        base = pl.multiple_of(c * R, R)
        for half in range(2):
            at = pl.ds(base + half * H, H)
            a_v[at, :] = jnp.where(drop, 0.0, a_v[at, :]) - change[:, half * width:(half + 1) * width]

        @pl.when(jnp.logical_and(p == 0, c == 0))
        def _():
            a_v[:B, :] = head[...]

    paired = min(done, n - done)

    @pl.loop(0, paired)
    def _(i):
        forward(done + i)
        update(2 * i)
        update(2 * i + 1)

    @pl.loop(2 * paired, n)
    def _(c):
        @pl.when(c >= done + paired)
        def _():
            forward(c)

        update(c)

    @pl.when(q < last)
    def _():
        @pl.loop(0, n)
        def _(c):
            hop(c).wait_send()

    @pl.when(p == 0)
    def _():
        for i in range(1, n_row):
            send_corner(i).wait_send()

    @pl.when(owner)
    def _():
        for i in range(1, n_row):
            send_cols(i, mine).wait_send()


def write_out(x_ref, o_ref, sems):
    n = sems.shape[0]
    step = x_ref.shape[0] // n
    copies = []
    for i in range(n):
        at = pl.ds(i * step, step)
        copies.append(pltpu.make_async_copy(x_ref.at[at], o_ref.at[at], sems.at[i]))
        copies[-1].start()
    for copy in copies:
        copy.wait()


def solution(mesh):
    n_row, n_col = mesh.shape["row"], mesh.shape["col"]

    def step(matrix):
        rows, width = matrix.shape
        n = rows // R
        per = n_row // n_col
        assert rows % R == 0 and n_row % n_col == 0 and width // B // per * B <= R
        updated = pl.pallas_call(
            functools.partial(kernel, n_row, n_col),
            out_shape=jax.ShapeDtypeStruct((rows, width), jnp.float32),
            in_specs=[pl.BlockSpec(memory_space=pltpu.HBM)],
            out_specs=pl.BlockSpec(memory_space=pltpu.VMEM),
            scratch_shapes=[
                pltpu.VMEM((rows // 2, LANES), jnp.float32),
                pltpu.VMEM((B, LANES), jnp.float32),
                pltpu.VMEM((per, H, LANES), jnp.float32),
                pltpu.VMEM((LANES, 2 * width), jnp.float32),
                pltpu.VMEM((B, width), jnp.float32),
                pltpu.SemaphoreType.DMA((n,)),
                pltpu.SemaphoreType.DMA((n,)),
                pltpu.SemaphoreType.DMA((n,)),
                pltpu.SemaphoreType.DMA((n_row - 1,)),
                pltpu.SemaphoreType.DMA((1,)),
                pltpu.SemaphoreType.DMA((n_row - 1,)),
                pltpu.SemaphoreType.DMA((per,)),
            ],
            compiler_params=pltpu.CompilerParams(
                collective_id=0, has_side_effects=True, vmem_limit_bytes=24 * 1024 * 1024
            ),
        )(pltpu.with_memory_space_constraint(matrix, pltpu.HBM))
        return pl.pallas_call(
            write_out,
            out_shape=pltpu.HBM((rows, width), jnp.float32),
            in_specs=[pl.BlockSpec(memory_space=pltpu.VMEM)],
            out_specs=pl.BlockSpec(memory_space=pltpu.HBM),
            scratch_shapes=[pltpu.SemaphoreType.DMA((5,))],
            compiler_params=pltpu.CompilerParams(vmem_limit_bytes=24 * 1024 * 1024),
        )(pltpu.with_memory_space_constraint(updated, pltpu.VMEM))

    return jax.shard_map(
        step, mesh=mesh, in_specs=(P("row", "col"),), out_specs=P("row", "col"), check_vma=False
    )
```

```python
import functools

import jax
import jax.numpy as jnp
from jax import lax
from jax.experimental import pallas as pl
from jax.experimental.pallas import tpu as pltpu
from jax.sharding import PartitionSpec as P

B = 64
R = 256
H = R // 2
LANES = 128
GROUP = 8
SPLIT = 2
S = H // SPLIT
LEAD = 3
EARLY = 2
MESH = pl.DeviceIdType.MESH
HI = lax.Precision.HIGHEST


def mm(a, b, contract):
    return lax.dot_general(
        a, b, ((contract[:1], contract[1:]), ((), ())), precision=HI, preferred_element_type=jnp.float32
    )


def kernel(n_row, n_col, a_ref, a_v, pack, corner_b, cols_b, m_b, head,
           a_in, f_send, f_recv, k_send, k_recv, c_send, c_recv):
    p = lax.axis_index("row")
    q = lax.axis_index("col")
    rows, width = a_v.shape
    n = rows // R
    per = n_row // n_col
    last = n_col - 1

    def fetch(c):
        at = pl.ds(pl.multiple_of(c * R, R), R)
        return pltpu.make_async_copy(a_ref.at[at], a_v.at[at], a_in.at[c])

    def hop(c):
        at = pl.ds(pl.multiple_of(c * S, S), S)
        return pltpu.make_async_remote_copy(
            src_ref=pack.at[at], dst_ref=pack.at[at], send_sem=f_send.at[c], recv_sem=f_recv.at[c],
            device_id=(p, lax.rem(q + 1, n_col)), device_id_type=MESH,
        )

    def peer(i):
        return lax.rem(p + i, n_row), q

    def send_corner(i):
        return pltpu.make_async_remote_copy(
            src_ref=pack.at[pl.ds(0, B)], dst_ref=corner_b, send_sem=k_send.at[i - 1], recv_sem=k_recv.at[0],
            device_id=peer(i), device_id_type=MESH,
        )

    def send_cols(i, slot):
        return pltpu.make_async_remote_copy(
            src_ref=pack.at[pl.ds(0, H)], dst_ref=cols_b.at[slot], send_sem=c_send.at[i - 1],
            recv_sem=c_recv.at[slot], device_id=peer(i), device_id_type=MESH,
        )

    for c in range(n):
        fetch(c).start()

    barrier = pltpu.get_barrier_semaphore()
    for i in range(1, n_row):
        pl.semaphore_signal(barrier, inc=1, device_id=peer(i), device_id_type=MESH)

    @pl.when(q > 0)
    def _():
        pl.semaphore_signal(barrier, inc=1, device_id=(p, q - 1), device_id_type=MESH)

    @pl.when(q < last)
    def _():
        pl.semaphore_signal(barrier, inc=1, device_id=(p, q + 1), device_id_type=MESH)

    ends = jnp.where(q > 0, 1, 0) + jnp.where(q < last, 1, 0)
    pl.semaphore_wait(barrier, n_row - 1 + ends)

    lane = lax.broadcasted_iota(jnp.int32, (H, LANES), 1)

    def source(c):
        fetch(c).wait()
        base = pl.multiple_of(c * R, R)
        top = a_v[pl.ds(base, H), :LANES]
        low = a_v[pl.ds(base + H, H), :LANES]
        pack[pl.ds(pl.multiple_of(c * H, H), H), :] = jnp.where(lane < B, top, pltpu.roll(low, B, 1))
        for part in range(SPLIT):
            hop(c * SPLIT + part).start()

    def forward(c):
        @pl.when(q > 0)
        def _():
            fetch(c).wait()
            for part in range(SPLIT):
                hop(c * SPLIT + part).wait_recv()

                @pl.when(q < last)
                def _(part=part):
                    hop(c * SPLIT + part).start()

    @pl.when(q == 0)
    def _():
        for c in range(min(EARLY, n)):
            source(c)

    forward(0)
    head[...] = a_v[:B, :]
    mine = p // n_col
    owner = lax.rem(p, n_col) == q

    @pl.when(p == 0)
    def _():
        for i in range(1, n_row):
            send_corner(i).start()
        corner_b[...] = pack[:B, :]

    @pl.when(owner)
    def _():
        for i in range(1, n_row):
            send_cols(i, mine).start()
        cols_b[mine] = pack[:H, :]

    @pl.when(q == 0)
    def _():
        @pl.loop(min(EARLY, n), n)
        def _(c):
            source(c)

    done = 1
    while done < min(1 + LEAD, n):
        forward(done)
        done += 1

    @pl.when(p != 0)
    def _():
        send_corner(1).wait_recv()

    raw = corner_b[...][:, :B]
    corner = (raw + raw.T) / 2.0
    row64 = lax.broadcasted_iota(jnp.int32, (B, B), 0)
    col64 = lax.broadcasted_iota(jnp.int32, (B, B), 1)
    eye = jnp.where(row64 == col64, 1.0, 0.0)
    aug = jnp.concatenate([corner, eye], axis=1)
    row_id = lax.broadcasted_iota(jnp.int32, (B, 1), 0)
    for k in range(B):
        scale = 1.0 / aug[k:k + 1, k:k + 1]
        weight = jnp.where(row_id > k, aug[:, k:k + 1] * scale, 0.0)
        aug = aug - weight * aug[k:k + 1, :]
        if k % GROUP == GROUP - 1 and done < n:
            forward(done)
            done += 1
    pivots = jnp.sum(jnp.where(row64 == col64, aug[:, :B], 0.0), axis=1, keepdims=True)
    inv = pltpu.roll(aug, B, 1)[:, :B] / jnp.sqrt(pivots)
    inv_t = inv.T
    sinv = mm(inv_t, inv, (1, 0))

    for slot in range(per):
        @pl.when(p != q + slot * n_col)
        def _(slot=slot):
            send_cols(1, slot).wait_recv()

    tiles = []
    for j in range(width // B):
        at = j // per * B
        block = cols_b[j % per, at % H:at % H + B, :]
        if at >= H:
            block = pltpu.roll(block, B, 1)
        tiles.append(block[:, :B])
    m = mm(sinv, jnp.concatenate(tiles, axis=0), (1, 1))
    first = q == 0
    m_first = jnp.where(first, -inv_t, m[:, :B])
    m = jnp.concatenate([m_first, m[:, B:]], axis=1)
    m_hi = m.astype(jnp.bfloat16)
    m_lo = (m - m_hi.astype(jnp.float32)).astype(jnp.bfloat16)
    m_b[...] = jnp.zeros_like(m_b)
    for i, term in enumerate((m_hi, m_hi, m_lo)):
        m_b[i * LANES:i * LANES + B, :width] = term
        m_b[i * LANES + B:(i + 1) * LANES, width:] = term
    factor = jnp.where(row64 >= col64, mm(corner, inv_t, (1, 0)), 0.0)
    head[:, :B] = jnp.where(first, factor, head[:, :B])
    wide = lax.broadcasted_iota(jnp.int32, (H, width), 1)
    drop = jnp.logical_and(first, wide < B)

    def update(c):
        rows_c = pack[pl.ds(pl.multiple_of(c * H, H), H), :]
        hi = rows_c.astype(jnp.bfloat16)
        lo = (rows_c - hi.astype(jnp.float32)).astype(jnp.bfloat16)
        change = jnp.dot(
            jnp.concatenate([hi, lo, hi], axis=1), m_b[...], preferred_element_type=jnp.float32
        )
        base = pl.multiple_of(c * R, R)
        for half in range(2):
            at = pl.ds(base + half * H, H)
            a_v[at, :] = jnp.where(drop, 0.0, a_v[at, :]) - change[:, half * width:(half + 1) * width]

        @pl.when(jnp.logical_and(p == 0, c == 0))
        def _():
            a_v[:B, :] = head[...]

    paired = min(done, n - done)

    @pl.loop(0, paired)
    def _(i):
        forward(done + i)
        update(2 * i)
        update(2 * i + 1)

    @pl.loop(2 * paired, n)
    def _(c):
        @pl.when(c >= done + paired)
        def _():
            forward(c)

        update(c)

    @pl.when(q < last)
    def _():
        @pl.loop(0, n * SPLIT)
        def _(c):
            hop(c).wait_send()

    @pl.when(p == 0)
    def _():
        for i in range(1, n_row):
            send_corner(i).wait_send()

    @pl.when(owner)
    def _():
        for i in range(1, n_row):
            send_cols(i, mine).wait_send()


def write_out(x_ref, o_ref, sems):
    n = sems.shape[0]
    step = x_ref.shape[0] // n
    copies = []
    for i in range(n):
        at = pl.ds(i * step, step)
        copies.append(pltpu.make_async_copy(x_ref.at[at], o_ref.at[at], sems.at[i]))
        copies[-1].start()
    for copy in copies:
        copy.wait()


def solution(mesh):
    n_row, n_col = mesh.shape["row"], mesh.shape["col"]

    def step(matrix):
        rows, width = matrix.shape
        n = rows // R
        per = n_row // n_col
        assert rows % R == 0 and n_row % n_col == 0 and width // B // per * B <= R
        updated = pl.pallas_call(
            functools.partial(kernel, n_row, n_col),
            out_shape=jax.ShapeDtypeStruct((rows, width), jnp.float32),
            in_specs=[pl.BlockSpec(memory_space=pltpu.HBM)],
            out_specs=pl.BlockSpec(memory_space=pltpu.VMEM),
            scratch_shapes=[
                pltpu.VMEM((rows // 2, LANES), jnp.float32),
                pltpu.VMEM((B, LANES), jnp.float32),
                pltpu.VMEM((per, H, LANES), jnp.float32),
                pltpu.VMEM((3 * LANES, 2 * width), jnp.bfloat16),
                pltpu.VMEM((B, width), jnp.float32),
                pltpu.SemaphoreType.DMA((n,)),
                pltpu.SemaphoreType.DMA((n * SPLIT,)),
                pltpu.SemaphoreType.DMA((n * SPLIT,)),
                pltpu.SemaphoreType.DMA((n_row - 1,)),
                pltpu.SemaphoreType.DMA((1,)),
                pltpu.SemaphoreType.DMA((n_row - 1,)),
                pltpu.SemaphoreType.DMA((per,)),
            ],
            compiler_params=pltpu.CompilerParams(
                collective_id=0, has_side_effects=True, vmem_limit_bytes=24 * 1024 * 1024
            ),
        )(pltpu.with_memory_space_constraint(matrix, pltpu.HBM))
        return pl.pallas_call(
            write_out,
            out_shape=pltpu.HBM((rows, width), jnp.float32),
            in_specs=[pl.BlockSpec(memory_space=pltpu.VMEM)],
            out_specs=pl.BlockSpec(memory_space=pltpu.HBM),
            scratch_shapes=[pltpu.SemaphoreType.DMA((5,))],
            compiler_params=pltpu.CompilerParams(vmem_limit_bytes=24 * 1024 * 1024),
        )(pltpu.with_memory_space_constraint(updated, pltpu.VMEM))

    return jax.shard_map(
        step, mesh=mesh, in_specs=(P("row", "col"),), out_specs=P("row", "col"), check_vma=False
    )
```

```python
import functools

import jax
import jax.numpy as jnp
from jax import lax
from jax.experimental import pallas as pl
from jax.experimental.pallas import tpu as pltpu
from jax.sharding import PartitionSpec as P

B = 64
R = 256
H = R // 2
LANES = 128
GROUP = 4
SPLIT = 2
S = H // SPLIT
LEAD = 4
EARLY = 2
MESH = pl.DeviceIdType.MESH
HI = lax.Precision.HIGHEST


def mm(a, b, contract):
    return lax.dot_general(
        a, b, ((contract[:1], contract[1:]), ((), ())), precision=HI, preferred_element_type=jnp.float32
    )


def kernel(n_row, n_col, a_ref, a_v, pack, corner_b, cols_b, m_b, head,
           a_in, f_send, f_recv, k_send, k_recv, c_send, c_recv):
    p = lax.axis_index("row")
    q = lax.axis_index("col")
    rows, width = a_v.shape
    n = rows // R
    per = n_row // n_col
    last = n_col - 1

    def fetch(c):
        at = pl.ds(pl.multiple_of(c * R, R), R)
        return pltpu.make_async_copy(a_ref.at[at], a_v.at[at], a_in.at[c])

    def hop(c):
        at = pl.ds(pl.multiple_of(c * S, S), S)
        return pltpu.make_async_remote_copy(
            src_ref=pack.at[at], dst_ref=pack.at[at], send_sem=f_send.at[c], recv_sem=f_recv.at[c],
            device_id=(p, lax.rem(q + 1, n_col)), device_id_type=MESH,
        )

    def peer(i):
        return lax.rem(p + i, n_row), q

    def send_corner(i):
        return pltpu.make_async_remote_copy(
            src_ref=pack.at[pl.ds(0, B)], dst_ref=corner_b, send_sem=k_send.at[i - 1], recv_sem=k_recv.at[0],
            device_id=peer(i), device_id_type=MESH,
        )

    def send_cols(i, slot):
        return pltpu.make_async_remote_copy(
            src_ref=pack.at[pl.ds(0, H)], dst_ref=cols_b.at[slot], send_sem=c_send.at[i - 1],
            recv_sem=c_recv.at[slot], device_id=peer(i), device_id_type=MESH,
        )

    barrier = pltpu.get_barrier_semaphore()

    @pl.when(q > 0)
    def _():
        pl.semaphore_signal(barrier, inc=1, device_id=(p, q - 1), device_id_type=MESH)

    for i in range(1, n_row):
        pl.semaphore_signal(barrier, inc=1, device_id=peer(i), device_id_type=MESH)

    @pl.when(q < last)
    def _():
        pl.semaphore_signal(barrier, inc=1, device_id=(p, q + 1), device_id_type=MESH)

    early = min(EARLY, n)
    for c in range(early):
        fetch(c).start()

    ends = jnp.where(q > 0, 1, 0) + jnp.where(q < last, 1, 0)
    pl.semaphore_wait(barrier, n_row - 1 + ends)

    lane = lax.broadcasted_iota(jnp.int32, (H, LANES), 1)

    def source(c):
        fetch(c).wait()
        base = pl.multiple_of(c * R, R)
        top = a_v[pl.ds(base, H), :LANES]
        low = a_v[pl.ds(base + H, H), :LANES]
        pack[pl.ds(pl.multiple_of(c * H, H), H), :] = jnp.where(lane < B, top, pltpu.roll(low, B, 1))
        for part in range(SPLIT):
            hop(c * SPLIT + part).start()

    def forward(h):
        @pl.when(q > 0)
        def _():
            hop(h).wait_recv()

            @pl.when(q < last)
            def _():
                hop(h).start()

    parts = n * SPLIT
    sent = 0

    def advance(count):
        nonlocal sent
        for _ in range(min(count, parts - sent)):
            forward(sent)
            sent += 1

    @pl.when(q == 0)
    def _():
        for c in range(early):
            source(c)

    @pl.loop(early, n)
    def _(c):
        fetch(c).start()

    advance(SPLIT)

    @pl.when(q > 0)
    def _():
        fetch(0).wait()

    head[...] = a_v[:B, :]
    mine = p // n_col
    owner = lax.rem(p, n_col) == q

    @pl.when(p == 0)
    def _():
        for i in range(1, n_row):
            send_corner(i).start()
        corner_b[...] = pack[:B, :]

    @pl.when(owner)
    def _():
        for i in range(1, n_row):
            send_cols(i, mine).start()
        cols_b[mine] = pack[:H, :]

    @pl.when(q == 0)
    def _():
        @pl.loop(early, n)
        def _(c):
            source(c)

    advance(LEAD)

    @pl.when(p != 0)
    def _():
        send_corner(1).wait_recv()

    raw = corner_b[...][:, :B]
    corner = (raw + raw.T) / 2.0
    row64 = lax.broadcasted_iota(jnp.int32, (B, B), 0)
    col64 = lax.broadcasted_iota(jnp.int32, (B, B), 1)
    eye = jnp.where(row64 == col64, 1.0, 0.0)
    aug = jnp.concatenate([corner, eye], axis=1)
    row_id = lax.broadcasted_iota(jnp.int32, (B, 1), 0)
    for k in range(B):
        scale = 1.0 / aug[k:k + 1, k:k + 1]
        weight = jnp.where(row_id > k, aug[:, k:k + 1] * scale, 0.0)
        aug = aug - weight * aug[k:k + 1, :]
        if k % GROUP == GROUP - 1:
            advance(1)
    pivots = jnp.sum(jnp.where(row64 == col64, aug[:, :B], 0.0), axis=1, keepdims=True)
    inv = pltpu.roll(aug, B, 1)[:, :B] / jnp.sqrt(pivots)
    inv_t = inv.T
    advance(1)
    sinv = mm(inv_t, inv, (1, 0))

    for slot in range(per):
        @pl.when(p != q + slot * n_col)
        def _(slot=slot):
            send_cols(1, slot).wait_recv()

    tiles = []
    for j in range(width // B):
        at = j // per * B
        block = cols_b[j % per, at % H:at % H + B, :]
        if at >= H:
            block = pltpu.roll(block, B, 1)
        tiles.append(block[:, :B])
    advance(1)
    m = mm(sinv, jnp.concatenate(tiles, axis=0), (1, 1))
    advance(1)
    first = q == 0
    m_first = jnp.where(first, -inv_t, m[:, :B])
    m = jnp.concatenate([m_first, m[:, B:]], axis=1)
    m_hi = m.astype(jnp.bfloat16)
    m_lo = (m - m_hi.astype(jnp.float32)).astype(jnp.bfloat16)
    m_b[...] = jnp.zeros_like(m_b)
    for i, term in enumerate((m_hi, m_hi, m_lo)):
        m_b[i * LANES:i * LANES + B, :width] = term
        m_b[i * LANES + B:(i + 1) * LANES, width:] = term
    advance(1)
    factor = jnp.where(row64 >= col64, mm(corner, inv_t, (1, 0)), 0.0)
    head[:, :B] = jnp.where(first, factor, head[:, :B])
    wide = lax.broadcasted_iota(jnp.int32, (H, width), 1)
    drop = jnp.logical_and(first, wide < B)

    def update(c):
        @pl.when(jnp.logical_and(q > 0, c > 0))
        def _():
            fetch(c).wait()

        rows_c = pack[pl.ds(pl.multiple_of(c * H, H), H), :]
        hi = rows_c.astype(jnp.bfloat16)
        lo = (rows_c - hi.astype(jnp.float32)).astype(jnp.bfloat16)
        change = jnp.dot(
            jnp.concatenate([hi, lo, hi], axis=1), m_b[...], preferred_element_type=jnp.float32
        )
        base = pl.multiple_of(c * R, R)
        for half in range(2):
            at = pl.ds(base + half * H, H)
            a_v[at, :] = jnp.where(drop, 0.0, a_v[at, :]) - change[:, half * width:(half + 1) * width]

        @pl.when(jnp.logical_and(p == 0, c == 0))
        def _():
            a_v[:B, :] = head[...]

    step = SPLIT // 2
    behind = min(sent // step, (parts - sent) // step)
    caught = behind * step == sent

    @pl.loop(0, behind)
    def _(c):
        for part in range(step):
            forward(sent + c * step + part)
        update(c)

    @pl.loop(behind, n)
    def _(c):
        if caught:
            for part in range(SPLIT):
                forward(c * SPLIT + part)
        update(c)

    @pl.when(q < last)
    def _():
        @pl.loop(0, n * SPLIT)
        def _(c):
            hop(c).wait_send()

    @pl.when(p == 0)
    def _():
        for i in range(1, n_row):
            send_corner(i).wait_send()

    @pl.when(owner)
    def _():
        for i in range(1, n_row):
            send_cols(i, mine).wait_send()


def write_out(x_ref, o_ref, sems):
    n = sems.shape[0]
    step = x_ref.shape[0] // n
    copies = []
    for i in range(n):
        at = pl.ds(i * step, step)
        copies.append(pltpu.make_async_copy(x_ref.at[at], o_ref.at[at], sems.at[i]))
        copies[-1].start()
    for copy in copies:
        copy.wait()


def solution(mesh):
    n_row, n_col = mesh.shape["row"], mesh.shape["col"]

    def step(matrix):
        rows, width = matrix.shape
        n = rows // R
        per = n_row // n_col
        assert rows % R == 0 and n_row % n_col == 0 and width // B // per * B <= R
        updated = pl.pallas_call(
            functools.partial(kernel, n_row, n_col),
            out_shape=jax.ShapeDtypeStruct((rows, width), jnp.float32),
            in_specs=[pl.BlockSpec(memory_space=pltpu.HBM)],
            out_specs=pl.BlockSpec(memory_space=pltpu.VMEM),
            scratch_shapes=[
                pltpu.VMEM((rows // 2, LANES), jnp.float32),
                pltpu.VMEM((B, LANES), jnp.float32),
                pltpu.VMEM((per, H, LANES), jnp.float32),
                pltpu.VMEM((3 * LANES, 2 * width), jnp.bfloat16),
                pltpu.VMEM((B, width), jnp.float32),
                pltpu.SemaphoreType.DMA((n,)),
                pltpu.SemaphoreType.DMA((n * SPLIT,)),
                pltpu.SemaphoreType.DMA((n * SPLIT,)),
                pltpu.SemaphoreType.DMA((n_row - 1,)),
                pltpu.SemaphoreType.DMA((1,)),
                pltpu.SemaphoreType.DMA((n_row - 1,)),
                pltpu.SemaphoreType.DMA((per,)),
            ],
            compiler_params=pltpu.CompilerParams(
                collective_id=0, has_side_effects=True, vmem_limit_bytes=24 * 1024 * 1024
            ),
        )(pltpu.with_memory_space_constraint(matrix, pltpu.HBM))
        return pl.pallas_call(
            write_out,
            out_shape=pltpu.HBM((rows, width), jnp.float32),
            in_specs=[pl.BlockSpec(memory_space=pltpu.VMEM)],
            out_specs=pl.BlockSpec(memory_space=pltpu.HBM),
            scratch_shapes=[pltpu.SemaphoreType.DMA((5,))],
            compiler_params=pltpu.CompilerParams(vmem_limit_bytes=24 * 1024 * 1024),
        )(pltpu.with_memory_space_constraint(updated, pltpu.VMEM))

    return jax.shard_map(
        step, mesh=mesh, in_specs=(P("row", "col"),), out_specs=P("row", "col"), check_vma=False
    )
```

```python
import functools

import jax
import jax.numpy as jnp
from jax import lax
from jax.experimental import pallas as pl
from jax.experimental.pallas import tpu as pltpu
from jax.sharding import PartitionSpec as P

B = 64
R = 256
H = R // 2
LANES = 128
GROUP = 4
SPLIT = 2
S = H // SPLIT
LEAD = 6
EARLY = 2
MESH = pl.DeviceIdType.MESH
HI = lax.Precision.HIGHEST


def mm(a, b, contract):
    return lax.dot_general(
        a, b, ((contract[:1], contract[1:]), ((), ())), precision=HI, preferred_element_type=jnp.float32
    )


def kernel(n_row, n_col, a_ref, a_v, pack, corner_b, cols_b, m_b, head,
           a_in, f_send, f_recv, k_send, k_recv, c_send, c_recv):
    p = lax.axis_index("row")
    q = lax.axis_index("col")
    rows, width = a_v.shape
    n = rows // R
    per = n_row // n_col
    last = n_col - 1

    def fetch(c):
        at = pl.ds(pl.multiple_of(c * R, R), R)
        return pltpu.make_async_copy(a_ref.at[at], a_v.at[at], a_in.at[c])

    def hop(c):
        at = pl.ds(pl.multiple_of(c * S, S), S)
        return pltpu.make_async_remote_copy(
            src_ref=pack.at[at], dst_ref=pack.at[at], send_sem=f_send.at[c], recv_sem=f_recv.at[c],
            device_id=(p, lax.rem(q + 1, n_col)), device_id_type=MESH,
        )

    def peer(i):
        return lax.rem(p + i, n_row), q

    def send_corner(i):
        return pltpu.make_async_remote_copy(
            src_ref=pack.at[pl.ds(0, B)], dst_ref=corner_b, send_sem=k_send.at[i - 1], recv_sem=k_recv.at[0],
            device_id=peer(i), device_id_type=MESH,
        )

    def send_cols(i, slot):
        return pltpu.make_async_remote_copy(
            src_ref=pack.at[pl.ds(0, H)], dst_ref=cols_b.at[slot], send_sem=c_send.at[i - 1],
            recv_sem=c_recv.at[slot], device_id=peer(i), device_id_type=MESH,
        )

    barrier = pltpu.get_barrier_semaphore()

    @pl.when(q > 0)
    def _():
        pl.semaphore_signal(barrier, inc=1, device_id=(p, q - 1), device_id_type=MESH)

    for i in range(1, n_row):
        pl.semaphore_signal(barrier, inc=1, device_id=peer(i), device_id_type=MESH)

    @pl.when(q < last)
    def _():
        pl.semaphore_signal(barrier, inc=1, device_id=(p, q + 1), device_id_type=MESH)

    early = min(EARLY, n)
    for c in range(early):
        fetch(c).start()

    ends = jnp.where(q > 0, 1, 0) + jnp.where(q < last, 1, 0)
    pl.semaphore_wait(barrier, n_row - 1 + ends)

    lane = lax.broadcasted_iota(jnp.int32, (H, LANES), 1)

    def source(c):
        fetch(c).wait()
        base = pl.multiple_of(c * R, R)
        top = a_v[pl.ds(base, H), :LANES]
        low = a_v[pl.ds(base + H, H), :LANES]
        pack[pl.ds(pl.multiple_of(c * H, H), H), :] = jnp.where(lane < B, top, pltpu.roll(low, B, 1))
        for part in range(SPLIT):
            hop(c * SPLIT + part).start()

    def forward(h):
        @pl.when(q > 0)
        def _():
            hop(h).wait_recv()

            @pl.when(q < last)
            def _():
                hop(h).start()

    parts = n * SPLIT
    sent = 0

    def advance(count):
        nonlocal sent
        for _ in range(min(count, parts - sent)):
            forward(sent)
            sent += 1

    @pl.when(q == 0)
    def _():
        for c in range(early):
            source(c)

    @pl.loop(early, n)
    def _(c):
        fetch(c).start()

    advance(SPLIT)

    @pl.when(q > 0)
    def _():
        fetch(0).wait()

    head[...] = a_v[:B, :]
    mine = p // n_col
    owner = lax.rem(p, n_col) == q

    @pl.when(p == 0)
    def _():
        for i in range(1, n_row):
            send_corner(i).start()
        corner_b[...] = pack[:B, :]

    advance(2)

    @pl.when(owner)
    def _():
        for i in range(1, n_row):
            send_cols(i, mine).start()
        cols_b[mine] = pack[:H, :]

    @pl.when(q == 0)
    def _():
        @pl.loop(early, n)
        def _(c):
            source(c)

    advance(LEAD)

    @pl.when(p != 0)
    def _():
        send_corner(1).wait_recv()

    raw = corner_b[...][:, :B]
    corner = (raw + raw.T) / 2.0
    row64 = lax.broadcasted_iota(jnp.int32, (B, B), 0)
    col64 = lax.broadcasted_iota(jnp.int32, (B, B), 1)
    eye = jnp.where(row64 == col64, 1.0, 0.0)
    aug = jnp.concatenate([corner, eye], axis=1)
    row_id = lax.broadcasted_iota(jnp.int32, (B, 1), 0)
    for k in range(B):
        scale = 1.0 / aug[k:k + 1, k:k + 1]
        weight = jnp.where(row_id > k, aug[:, k:k + 1] * scale, 0.0)
        aug = aug - weight * aug[k:k + 1, :]
        if k % GROUP == GROUP - 1:
            advance(1)
    pivots = jnp.sum(jnp.where(row64 == col64, aug[:, :B], 0.0), axis=1, keepdims=True)
    inv = pltpu.roll(aug, B, 1)[:, :B] / jnp.sqrt(pivots)
    inv_t = inv.T
    advance(1)
    sinv = mm(inv_t, inv, (1, 0))

    for slot in range(per):
        @pl.when(p != q + slot * n_col)
        def _(slot=slot):
            send_cols(1, slot).wait_recv()

    tiles = []
    for j in range(width // B):
        at = j // per * B
        block = cols_b[j % per, at % H:at % H + B, :]
        if at >= H:
            block = pltpu.roll(block, B, 1)
        tiles.append(block[:, :B])
    advance(1)
    m = mm(sinv, jnp.concatenate(tiles, axis=0), (1, 1))
    advance(1)
    first = q == 0
    m_first = jnp.where(first, -inv_t, m[:, :B])
    m = jnp.concatenate([m_first, m[:, B:]], axis=1)
    m_hi = m.astype(jnp.bfloat16)
    m_lo = (m - m_hi.astype(jnp.float32)).astype(jnp.bfloat16)
    m_b[...] = jnp.zeros_like(m_b)
    for i, term in enumerate((m_hi, m_hi, m_lo)):
        m_b[i * LANES:i * LANES + B, :width] = term
        m_b[i * LANES + B:(i + 1) * LANES, width:] = term
    advance(1)
    factor = jnp.where(row64 >= col64, mm(corner, inv_t, (1, 0)), 0.0)
    head[:, :B] = jnp.where(first, factor, head[:, :B])
    wide = lax.broadcasted_iota(jnp.int32, (H, width), 1)
    drop = jnp.logical_and(first, wide < B)

    def update(c):
        @pl.when(jnp.logical_and(q > 0, c > 0))
        def _():
            fetch(c).wait()

        rows_c = pack[pl.ds(pl.multiple_of(c * H, H), H), :]
        hi = rows_c.astype(jnp.bfloat16)
        lo = (rows_c - hi.astype(jnp.float32)).astype(jnp.bfloat16)
        change = jnp.dot(
            jnp.concatenate([hi, lo, hi], axis=1), m_b[...], preferred_element_type=jnp.float32
        )
        base = pl.multiple_of(c * R, R)
        for half in range(2):
            at = pl.ds(base + half * H, H)
            a_v[at, :] = jnp.where(drop, 0.0, a_v[at, :]) - change[:, half * width:(half + 1) * width]

        @pl.when(jnp.logical_and(p == 0, c == 0))
        def _():
            a_v[:B, :] = head[...]

    step = SPLIT // 2
    behind = min(sent // step, (parts - sent) // step)
    caught = behind * step == sent

    @pl.loop(0, behind)
    def _(c):
        for part in range(step):
            forward(sent + c * step + part)
        update(c)

    @pl.loop(behind, n)
    def _(c):
        if caught:
            for part in range(SPLIT):
                forward(c * SPLIT + part)
        update(c)

    @pl.when(q < last)
    def _():
        @pl.loop(0, n * SPLIT)
        def _(c):
            hop(c).wait_send()

    @pl.when(p == 0)
    def _():
        for i in range(1, n_row):
            send_corner(i).wait_send()

    @pl.when(owner)
    def _():
        for i in range(1, n_row):
            send_cols(i, mine).wait_send()


def write_out(x_ref, o_ref, sems):
    n = sems.shape[0]
    step = x_ref.shape[0] // n
    copies = []
    for i in range(n):
        at = pl.ds(i * step, step)
        copies.append(pltpu.make_async_copy(x_ref.at[at], o_ref.at[at], sems.at[i]))
        copies[-1].start()
    for copy in copies:
        copy.wait()


def solution(mesh):
    n_row, n_col = mesh.shape["row"], mesh.shape["col"]

    def step(matrix):
        rows, width = matrix.shape
        n = rows // R
        per = n_row // n_col
        assert rows % R == 0 and n_row % n_col == 0 and width // B // per * B <= R
        updated = pl.pallas_call(
            functools.partial(kernel, n_row, n_col),
            out_shape=jax.ShapeDtypeStruct((rows, width), jnp.float32),
            in_specs=[pl.BlockSpec(memory_space=pltpu.HBM)],
            out_specs=pl.BlockSpec(memory_space=pltpu.VMEM),
            scratch_shapes=[
                pltpu.VMEM((rows // 2, LANES), jnp.float32),
                pltpu.VMEM((B, LANES), jnp.float32),
                pltpu.VMEM((per, H, LANES), jnp.float32),
                pltpu.VMEM((3 * LANES, 2 * width), jnp.bfloat16),
                pltpu.VMEM((B, width), jnp.float32),
                pltpu.SemaphoreType.DMA((n,)),
                pltpu.SemaphoreType.DMA((n * SPLIT,)),
                pltpu.SemaphoreType.DMA((n * SPLIT,)),
                pltpu.SemaphoreType.DMA((n_row - 1,)),
                pltpu.SemaphoreType.DMA((1,)),
                pltpu.SemaphoreType.DMA((n_row - 1,)),
                pltpu.SemaphoreType.DMA((per,)),
            ],
            compiler_params=pltpu.CompilerParams(
                collective_id=0, has_side_effects=True, vmem_limit_bytes=24 * 1024 * 1024
            ),
        )(pltpu.with_memory_space_constraint(matrix, pltpu.HBM))
        return pl.pallas_call(
            write_out,
            out_shape=pltpu.HBM((rows, width), jnp.float32),
            in_specs=[pl.BlockSpec(memory_space=pltpu.VMEM)],
            out_specs=pl.BlockSpec(memory_space=pltpu.HBM),
            scratch_shapes=[pltpu.SemaphoreType.DMA((5,))],
            compiler_params=pltpu.CompilerParams(vmem_limit_bytes=24 * 1024 * 1024),
        )(pltpu.with_memory_space_constraint(updated, pltpu.VMEM))

    return jax.shard_map(
        step, mesh=mesh, in_specs=(P("row", "col"),), out_specs=P("row", "col"), check_vma=False
    )
```

```python
import functools

import jax
import jax.numpy as jnp
from jax import lax
from jax.experimental import pallas as pl
from jax.experimental.pallas import tpu as pltpu
from jax.sharding import PartitionSpec as P

B = 64
R = 256
H = R // 2
LANES = 128
GROUP = 2
SPLIT = 4
S = H // SPLIT
LEAD = 12
EARLY = 2
MESH = pl.DeviceIdType.MESH
HI = lax.Precision.HIGHEST


def mm(a, b, contract):
    return lax.dot_general(
        a, b, ((contract[:1], contract[1:]), ((), ())), precision=HI, preferred_element_type=jnp.float32
    )


def kernel(n_row, n_col, a_ref, a_v, pack, corner_b, cols_b, m_b, head,
           a_in, f_send, f_recv, k_send, k_recv, c_send, c_recv):
    p = lax.axis_index("row")
    q = lax.axis_index("col")
    rows, width = a_v.shape
    n = rows // R
    per = n_row // n_col
    last = n_col - 1

    def fetch(c):
        at = pl.ds(pl.multiple_of(c * R, R), R)
        return pltpu.make_async_copy(a_ref.at[at], a_v.at[at], a_in.at[c])

    def hop(c):
        at = pl.ds(pl.multiple_of(c * S, S), S)
        return pltpu.make_async_remote_copy(
            src_ref=pack.at[at], dst_ref=pack.at[at], send_sem=f_send.at[c], recv_sem=f_recv.at[c],
            device_id=(p, lax.rem(q + 1, n_col)), device_id_type=MESH,
        )

    def peer(i):
        return lax.rem(p + i, n_row), q

    def send_corner(i):
        return pltpu.make_async_remote_copy(
            src_ref=pack.at[pl.ds(0, B)], dst_ref=corner_b, send_sem=k_send.at[i - 1], recv_sem=k_recv.at[0],
            device_id=peer(i), device_id_type=MESH,
        )

    def send_cols(i, slot):
        return pltpu.make_async_remote_copy(
            src_ref=pack.at[pl.ds(0, H)], dst_ref=cols_b.at[slot], send_sem=c_send.at[i - 1],
            recv_sem=c_recv.at[slot], device_id=peer(i), device_id_type=MESH,
        )

    barrier = pltpu.get_barrier_semaphore()

    @pl.when(q > 0)
    def _():
        pl.semaphore_signal(barrier, inc=1, device_id=(p, q - 1), device_id_type=MESH)

    for i in range(1, n_row):
        pl.semaphore_signal(barrier, inc=1, device_id=peer(i), device_id_type=MESH)

    @pl.when(q < last)
    def _():
        pl.semaphore_signal(barrier, inc=1, device_id=(p, q + 1), device_id_type=MESH)

    early = min(EARLY, n)
    for c in range(early):
        fetch(c).start()

    ends = jnp.where(q > 0, 1, 0) + jnp.where(q < last, 1, 0)
    pl.semaphore_wait(barrier, n_row - 1 + ends)

    lane = lax.broadcasted_iota(jnp.int32, (H, LANES), 1)

    def source(c):
        fetch(c).wait()
        base = pl.multiple_of(c * R, R)
        top = a_v[pl.ds(base, H), :LANES]
        low = a_v[pl.ds(base + H, H), :LANES]
        pack[pl.ds(pl.multiple_of(c * H, H), H), :] = jnp.where(lane < B, top, pltpu.roll(low, B, 1))
        for part in range(SPLIT):
            hop(c * SPLIT + part).start()

    def forward(h):
        @pl.when(q > 0)
        def _():
            hop(h).wait_recv()

            @pl.when(q < last)
            def _():
                hop(h).start()

    parts = n * SPLIT
    sent = 0

    def advance(count):
        nonlocal sent
        for _ in range(min(count, parts - sent)):
            forward(sent)
            sent += 1

    @pl.when(q == 0)
    def _():
        for c in range(early):
            source(c)

    @pl.loop(early, n)
    def _(c):
        fetch(c).start()

    advance(SPLIT)

    @pl.when(q > 0)
    def _():
        fetch(0).wait()

    head[...] = a_v[:B, :]
    mine = p // n_col
    owner = lax.rem(p, n_col) == q

    @pl.when(p == 0)
    def _():
        for i in range(1, n_row):
            send_corner(i).start()
        corner_b[...] = pack[:B, :]

    advance(4)

    @pl.when(owner)
    def _():
        for i in range(1, n_row):
            send_cols(i, mine).start()
        cols_b[mine] = pack[:H, :]

    @pl.when(q == 0)
    def _():
        @pl.loop(early, n)
        def _(c):
            source(c)

    advance(LEAD)

    @pl.when(p != 0)
    def _():
        send_corner(1).wait_recv()

    raw = corner_b[...][:, :B]
    corner = (raw + raw.T) / 2.0
    row64 = lax.broadcasted_iota(jnp.int32, (B, B), 0)
    col64 = lax.broadcasted_iota(jnp.int32, (B, B), 1)
    eye = jnp.where(row64 == col64, 1.0, 0.0)
    aug = jnp.concatenate([corner, eye], axis=1)
    blocks = [aug[i:i + 8] for i in range(0, B, 8)]
    row_id = lax.broadcasted_iota(jnp.int32, (8, 1), 0)
    for k in range(B):
        b, at = divmod(k, 8)
        row = blocks[b][at:at + 1, :]
        scaled = row / row[:, k:k + 1]
        for r in range(b, B // 8):
            weight = blocks[r][:, k:k + 1]
            if r == b:
                weight = jnp.where(row_id > at, weight, 0.0)
            blocks[r] = blocks[r] - weight * scaled
        if k % GROUP == GROUP - 1:
            advance(1)
    aug = jnp.concatenate(blocks, axis=0)
    pivots = jnp.sum(jnp.where(row64 == col64, aug[:, :B], 0.0), axis=1, keepdims=True)
    inv = pltpu.roll(aug, B, 1)[:, :B] / jnp.sqrt(pivots)
    inv_t = inv.T
    advance(2)
    sinv = mm(inv_t, inv, (1, 0))

    for slot in range(per):
        @pl.when(p != q + slot * n_col)
        def _(slot=slot):
            send_cols(1, slot).wait_recv()

    tiles = []
    for j in range(width // B):
        at = j // per * B
        block = cols_b[j % per, at % H:at % H + B, :]
        if at >= H:
            block = pltpu.roll(block, B, 1)
        tiles.append(block[:, :B])
    advance(2)
    m = mm(sinv, jnp.concatenate(tiles, axis=0), (1, 1))
    advance(2)
    first = q == 0
    m_first = jnp.where(first, -inv_t, m[:, :B])
    m = jnp.concatenate([m_first, m[:, B:]], axis=1)
    m_hi = m.astype(jnp.bfloat16)
    m_lo = (m - m_hi.astype(jnp.float32)).astype(jnp.bfloat16)
    m_b[...] = jnp.zeros_like(m_b)
    for i, term in enumerate((m_hi, m_hi, m_lo)):
        m_b[i * LANES:i * LANES + B, :width] = term
        m_b[i * LANES + B:(i + 1) * LANES, width:] = term
    advance(2)
    factor = jnp.where(row64 >= col64, mm(corner, inv_t, (1, 0)), 0.0)
    head[:, :B] = jnp.where(first, factor, head[:, :B])
    wide = lax.broadcasted_iota(jnp.int32, (H, width), 1)
    drop = jnp.logical_and(first, wide < B)

    def update(c):
        @pl.when(jnp.logical_and(q > 0, c > 0))
        def _():
            fetch(c).wait()

        rows_c = pack[pl.ds(pl.multiple_of(c * H, H), H), :]
        hi = rows_c.astype(jnp.bfloat16)
        lo = (rows_c - hi.astype(jnp.float32)).astype(jnp.bfloat16)
        change = jnp.dot(
            jnp.concatenate([hi, lo, hi], axis=1), m_b[...], preferred_element_type=jnp.float32
        )
        base = pl.multiple_of(c * R, R)
        for half in range(2):
            at = pl.ds(base + half * H, H)
            a_v[at, :] = jnp.where(drop, 0.0, a_v[at, :]) - change[:, half * width:(half + 1) * width]

        @pl.when(jnp.logical_and(p == 0, c == 0))
        def _():
            a_v[:B, :] = head[...]

    step = SPLIT // 2
    behind = min(sent // step, (parts - sent) // step)
    caught = behind * step == sent

    @pl.loop(0, behind)
    def _(c):
        for part in range(step):
            forward(sent + c * step + part)
        update(c)

    @pl.loop(behind, n)
    def _(c):
        if caught:
            for part in range(SPLIT):
                forward(c * SPLIT + part)
        update(c)

    @pl.when(q < last)
    def _():
        @pl.loop(0, n * SPLIT)
        def _(c):
            hop(c).wait_send()

    @pl.when(p == 0)
    def _():
        for i in range(1, n_row):
            send_corner(i).wait_send()

    @pl.when(owner)
    def _():
        for i in range(1, n_row):
            send_cols(i, mine).wait_send()


def write_out(x_ref, o_ref, sems):
    n = sems.shape[0]
    step = x_ref.shape[0] // n
    copies = []
    for i in range(n):
        at = pl.ds(i * step, step)
        copies.append(pltpu.make_async_copy(x_ref.at[at], o_ref.at[at], sems.at[i]))
        copies[-1].start()
    for copy in copies:
        copy.wait()


def solution(mesh):
    n_row, n_col = mesh.shape["row"], mesh.shape["col"]

    def step(matrix):
        rows, width = matrix.shape
        n = rows // R
        per = n_row // n_col
        assert rows % R == 0 and n_row % n_col == 0 and width // B // per * B <= R
        updated = pl.pallas_call(
            functools.partial(kernel, n_row, n_col),
            out_shape=jax.ShapeDtypeStruct((rows, width), jnp.float32),
            in_specs=[pl.BlockSpec(memory_space=pltpu.HBM)],
            out_specs=pl.BlockSpec(memory_space=pltpu.VMEM),
            scratch_shapes=[
                pltpu.VMEM((rows // 2, LANES), jnp.float32),
                pltpu.VMEM((B, LANES), jnp.float32),
                pltpu.VMEM((per, H, LANES), jnp.float32),
                pltpu.VMEM((3 * LANES, 2 * width), jnp.bfloat16),
                pltpu.VMEM((B, width), jnp.float32),
                pltpu.SemaphoreType.DMA((n,)),
                pltpu.SemaphoreType.DMA((n * SPLIT,)),
                pltpu.SemaphoreType.DMA((n * SPLIT,)),
                pltpu.SemaphoreType.DMA((n_row - 1,)),
                pltpu.SemaphoreType.DMA((1,)),
                pltpu.SemaphoreType.DMA((n_row - 1,)),
                pltpu.SemaphoreType.DMA((per,)),
            ],
            compiler_params=pltpu.CompilerParams(
                collective_id=0, has_side_effects=True, vmem_limit_bytes=24 * 1024 * 1024
            ),
        )(pltpu.with_memory_space_constraint(matrix, pltpu.HBM))
        return pl.pallas_call(
            write_out,
            out_shape=pltpu.HBM((rows, width), jnp.float32),
            in_specs=[pl.BlockSpec(memory_space=pltpu.VMEM)],
            out_specs=pl.BlockSpec(memory_space=pltpu.HBM),
            scratch_shapes=[pltpu.SemaphoreType.DMA((5,))],
            compiler_params=pltpu.CompilerParams(vmem_limit_bytes=24 * 1024 * 1024),
        )(pltpu.with_memory_space_constraint(updated, pltpu.VMEM))

    return jax.shard_map(
        step, mesh=mesh, in_specs=(P("row", "col"),), out_specs=P("row", "col"), check_vma=False
    )
```

```python
import functools

import jax
import jax.numpy as jnp
from jax import lax
from jax.experimental import pallas as pl
from jax.experimental.pallas import tpu as pltpu
from jax.sharding import PartitionSpec as P

B = 64
R = 256
H = R // 2
LANES = 128
GROUP = 4
SPLIT = 2
S = H // SPLIT
LEAD = 6
EARLY = 2
MESH = pl.DeviceIdType.MESH
HI = lax.Precision.HIGHEST


def mm(a, b, contract):
    return lax.dot_general(
        a, b, ((contract[:1], contract[1:]), ((), ())), precision=HI, preferred_element_type=jnp.float32
    )


def kernel(n_row, n_col, a_ref, a_v, pack, corner_b, cols_b, m_b, head,
           a_in, f_send, b_send, f_recv, k_send, k_recv, c_send, c_recv):
    p = lax.axis_index("row")
    q = lax.axis_index("col")
    rows, width = a_v.shape
    n = rows // R
    per = n_row // n_col
    mid = n_col // 2
    source_q = jnp.where(q == mid, 0, jnp.where(q > mid, q - 1, q + 1))
    target_q = jnp.where(q == 0, mid, lax.rem(q + 1, n_col))
    sends_on = jnp.logical_or(q == 0, jnp.logical_and(q >= mid, q < n_col - 1))
    sends_back = jnp.logical_and(q > 1, q <= mid)

    def fetch(c):
        at = pl.ds(pl.multiple_of(c * R, R), R)
        return pltpu.make_async_copy(a_ref.at[at], a_v.at[at], a_in.at[c])

    def hop(c):
        at = pl.ds(pl.multiple_of(c * S, S), S)
        return pltpu.make_async_remote_copy(
            src_ref=pack.at[at], dst_ref=pack.at[at], send_sem=f_send.at[c], recv_sem=f_recv.at[c],
            device_id=(p, target_q), device_id_type=MESH,
        )

    def hop_back(c):
        at = pl.ds(pl.multiple_of(c * S, S), S)
        return pltpu.make_async_remote_copy(
            src_ref=pack.at[at], dst_ref=pack.at[at], send_sem=b_send.at[c], recv_sem=f_recv.at[c],
            device_id=(p, lax.rem(q + n_col - 1, n_col)), device_id_type=MESH,
        )

    def peer(i):
        return lax.rem(p + i, n_row), q

    def send_corner(i):
        return pltpu.make_async_remote_copy(
            src_ref=pack.at[pl.ds(0, B)], dst_ref=corner_b, send_sem=k_send.at[i - 1], recv_sem=k_recv.at[0],
            device_id=peer(i), device_id_type=MESH,
        )

    def send_cols(i, slot):
        return pltpu.make_async_remote_copy(
            src_ref=pack.at[pl.ds(0, H)], dst_ref=cols_b.at[slot], send_sem=c_send.at[i - 1],
            recv_sem=c_recv.at[slot], device_id=peer(i), device_id_type=MESH,
        )

    barrier = pltpu.get_barrier_semaphore()

    @pl.when(q > 0)
    def _():
        pl.semaphore_signal(barrier, inc=1, device_id=(p, source_q), device_id_type=MESH)

    for i in range(1, n_row):
        pl.semaphore_signal(barrier, inc=1, device_id=peer(i), device_id_type=MESH)

    @pl.when(sends_on)
    def _():
        pl.semaphore_signal(barrier, inc=1, device_id=(p, target_q), device_id_type=MESH)

    @pl.when(sends_back)
    def _():
        pl.semaphore_signal(barrier, inc=1, device_id=(p, q - 1), device_id_type=MESH)

    early = min(EARLY, n)
    for c in range(early):
        fetch(c).start()

    ends = jnp.where(q > 0, 1, 0) + jnp.where(sends_on, 1, 0) + jnp.where(sends_back, 1, 0)
    pl.semaphore_wait(barrier, n_row - 1 + ends)

    lane = lax.broadcasted_iota(jnp.int32, (H, LANES), 1)

    def source(c):
        fetch(c).wait()
        base = pl.multiple_of(c * R, R)
        top = a_v[pl.ds(base, H), :LANES]
        low = a_v[pl.ds(base + H, H), :LANES]
        pack[pl.ds(pl.multiple_of(c * H, H), H), :] = jnp.where(lane < B, top, pltpu.roll(low, B, 1))
        for part in range(SPLIT):
            hop(c * SPLIT + part).start()

    def forward(h):
        @pl.when(q > 0)
        def _():
            hop(h).wait_recv()

            @pl.when(sends_on)
            def _():
                hop(h).start()

            @pl.when(sends_back)
            def _():
                hop_back(h).start()

    parts = n * SPLIT
    sent = 0

    def advance(count):
        nonlocal sent
        for _ in range(min(count, parts - sent)):
            forward(sent)
            sent += 1

    @pl.when(q == 0)
    def _():
        for c in range(early):
            source(c)

    @pl.loop(early, n)
    def _(c):
        fetch(c).start()

    advance(SPLIT)

    @pl.when(q > 0)
    def _():
        fetch(0).wait()

    head[...] = a_v[:B, :]
    mine = p // n_col
    owner = lax.rem(p, n_col) == q

    @pl.when(p == 0)
    def _():
        for i in range(1, n_row):
            send_corner(i).start()
        corner_b[...] = pack[:B, :]

    advance(2)

    @pl.when(owner)
    def _():
        for i in range(1, n_row):
            send_cols(i, mine).start()
        cols_b[mine] = pack[:H, :]

    @pl.when(q == 0)
    def _():
        @pl.loop(early, n)
        def _(c):
            source(c)

    advance(LEAD)

    @pl.when(p != 0)
    def _():
        send_corner(1).wait_recv()

    raw = corner_b[...][:, :B]
    corner = (raw + raw.T) / 2.0
    row64 = lax.broadcasted_iota(jnp.int32, (B, B), 0)
    col64 = lax.broadcasted_iota(jnp.int32, (B, B), 1)
    eye = jnp.where(row64 == col64, 1.0, 0.0)
    aug = jnp.concatenate([corner, eye], axis=1)
    blocks = [aug[i:i + 8] for i in range(0, B, 8)]
    row_id = lax.broadcasted_iota(jnp.int32, (8, 1), 0)
    for k in range(B):
        b, at = divmod(k, 8)
        row = blocks[b][at:at + 1, :]
        scaled = row / row[:, k:k + 1]
        for r in range(b, B // 8):
            weight = blocks[r][:, k:k + 1]
            if r == b:
                weight = jnp.where(row_id > at, weight, 0.0)
            blocks[r] = blocks[r] - weight * scaled
        if k % GROUP == GROUP - 1:
            advance(1)
    aug = jnp.concatenate(blocks, axis=0)
    pivots = jnp.sum(jnp.where(row64 == col64, aug[:, :B], 0.0), axis=1, keepdims=True)
    inv = pltpu.roll(aug, B, 1)[:, :B] / jnp.sqrt(pivots)
    inv_t = inv.T
    advance(1)
    sinv = mm(inv_t, inv, (1, 0))

    for slot in range(per):
        @pl.when(p != q + slot * n_col)
        def _(slot=slot):
            send_cols(1, slot).wait_recv()

    tiles = []
    for j in range(width // B):
        at = j // per * B
        block = cols_b[j % per, at % H:at % H + B, :]
        if at >= H:
            block = pltpu.roll(block, B, 1)
        tiles.append(block[:, :B])
    advance(1)
    m = mm(sinv, jnp.concatenate(tiles, axis=0), (1, 1))
    advance(1)
    first = q == 0
    m_first = jnp.where(first, -inv_t, m[:, :B])
    m = jnp.concatenate([m_first, m[:, B:]], axis=1)
    m_hi = m.astype(jnp.bfloat16)
    m_lo = (m - m_hi.astype(jnp.float32)).astype(jnp.bfloat16)
    m_b[...] = jnp.zeros_like(m_b)
    for i, term in enumerate((m_hi, m_hi, m_lo)):
        m_b[i * LANES:i * LANES + B, :width] = term
        m_b[i * LANES + B:(i + 1) * LANES, width:] = term
    advance(1)
    factor = jnp.where(row64 >= col64, mm(corner, inv_t, (1, 0)), 0.0)
    head[:, :B] = jnp.where(first, factor, head[:, :B])
    wide = lax.broadcasted_iota(jnp.int32, (H, width), 1)
    drop = jnp.logical_and(first, wide < B)

    def update(c):
        @pl.when(jnp.logical_and(q > 0, c > 0))
        def _():
            fetch(c).wait()

        rows_c = pack[pl.ds(pl.multiple_of(c * H, H), H), :]
        hi = rows_c.astype(jnp.bfloat16)
        lo = (rows_c - hi.astype(jnp.float32)).astype(jnp.bfloat16)
        change = jnp.dot(
            jnp.concatenate([hi, lo, hi], axis=1), m_b[...], preferred_element_type=jnp.float32
        )
        base = pl.multiple_of(c * R, R)
        for half in range(2):
            at = pl.ds(base + half * H, H)
            a_v[at, :] = jnp.where(drop, 0.0, a_v[at, :]) - change[:, half * width:(half + 1) * width]

        @pl.when(jnp.logical_and(p == 0, c == 0))
        def _():
            a_v[:B, :] = head[...]

    step = SPLIT // 2
    behind = min(sent // step, (parts - sent) // step)
    caught = behind * step == sent

    @pl.loop(0, behind)
    def _(c):
        for part in range(step):
            forward(sent + c * step + part)
        update(c)

    @pl.loop(behind, n)
    def _(c):
        if caught:
            for part in range(SPLIT):
                forward(c * SPLIT + part)
        update(c)

    @pl.when(sends_on)
    def _():
        @pl.loop(0, n * SPLIT)
        def _(c):
            hop(c).wait_send()

    @pl.when(sends_back)
    def _():
        @pl.loop(0, n * SPLIT)
        def _(c):
            hop_back(c).wait_send()

    @pl.when(p == 0)
    def _():
        for i in range(1, n_row):
            send_corner(i).wait_send()

    @pl.when(owner)
    def _():
        for i in range(1, n_row):
            send_cols(i, mine).wait_send()


def write_out(x_ref, o_ref, sems):
    n = sems.shape[0]
    step = x_ref.shape[0] // n
    copies = []
    for i in range(n):
        at = pl.ds(i * step, step)
        copies.append(pltpu.make_async_copy(x_ref.at[at], o_ref.at[at], sems.at[i]))
        copies[-1].start()
    for copy in copies:
        copy.wait()


def solution(mesh):
    n_row, n_col = mesh.shape["row"], mesh.shape["col"]

    def step(matrix):
        rows, width = matrix.shape
        n = rows // R
        per = n_row // n_col
        assert rows % R == 0 and n_row % n_col == 0 and width // B // per * B <= R
        updated = pl.pallas_call(
            functools.partial(kernel, n_row, n_col),
            out_shape=jax.ShapeDtypeStruct((rows, width), jnp.float32),
            in_specs=[pl.BlockSpec(memory_space=pltpu.HBM)],
            out_specs=pl.BlockSpec(memory_space=pltpu.VMEM),
            scratch_shapes=[
                pltpu.VMEM((rows // 2, LANES), jnp.float32),
                pltpu.VMEM((B, LANES), jnp.float32),
                pltpu.VMEM((per, H, LANES), jnp.float32),
                pltpu.VMEM((3 * LANES, 2 * width), jnp.bfloat16),
                pltpu.VMEM((B, width), jnp.float32),
                pltpu.SemaphoreType.DMA((n,)),
                pltpu.SemaphoreType.DMA((n * SPLIT,)),
                pltpu.SemaphoreType.DMA((n * SPLIT,)),
                pltpu.SemaphoreType.DMA((n * SPLIT,)),
                pltpu.SemaphoreType.DMA((n_row - 1,)),
                pltpu.SemaphoreType.DMA((1,)),
                pltpu.SemaphoreType.DMA((n_row - 1,)),
                pltpu.SemaphoreType.DMA((per,)),
            ],
            compiler_params=pltpu.CompilerParams(
                collective_id=0, has_side_effects=True, vmem_limit_bytes=24 * 1024 * 1024
            ),
        )(pltpu.with_memory_space_constraint(matrix, pltpu.HBM))
        return pl.pallas_call(
            write_out,
            out_shape=pltpu.HBM((rows, width), jnp.float32),
            in_specs=[pl.BlockSpec(memory_space=pltpu.VMEM)],
            out_specs=pl.BlockSpec(memory_space=pltpu.HBM),
            scratch_shapes=[pltpu.SemaphoreType.DMA((5,))],
            compiler_params=pltpu.CompilerParams(vmem_limit_bytes=24 * 1024 * 1024),
        )(pltpu.with_memory_space_constraint(updated, pltpu.VMEM))

    return jax.shard_map(
        step, mesh=mesh, in_specs=(P("row", "col"),), out_specs=P("row", "col"), check_vma=False
    )
```

```python
import functools

import jax
import jax.numpy as jnp
from jax import lax
from jax.experimental import pallas as pl
from jax.experimental.pallas import tpu as pltpu
from jax.sharding import PartitionSpec as P

B = 64
R = 256
H = R // 2
LANES = 128
GROUP = 4
SPLIT = 2
TAIL = 2
S = H // SPLIT
LEAD = 6
EARLY = 2
MESH = pl.DeviceIdType.MESH
HI = lax.Precision.HIGHEST


def mm(a, b, contract):
    return lax.dot_general(
        a, b, ((contract[:1], contract[1:]), ((), ())), precision=HI, preferred_element_type=jnp.float32
    )


def product(rows, m_ref):
    hi = rows.astype(jnp.bfloat16)
    lo = (rows - hi.astype(jnp.float32)).astype(jnp.bfloat16)
    return jnp.dot(jnp.concatenate([hi, lo, hi], axis=1), m_ref[...], preferred_element_type=jnp.float32)


def kernel(n_row, n_col, a_ref, a_v, pack, m_b, corner_b, cols_b, head,
           a_in, f_send, b_send, f_recv, k_send, k_recv, c_send, c_recv):
    p = lax.axis_index("row")
    q = lax.axis_index("col")
    rows, width = a_v.shape
    n = rows // R
    per = n_row // n_col
    mid = n_col // 2
    source_q = jnp.where(q == mid, 0, jnp.where(q > mid, q - 1, q + 1))
    target_q = jnp.where(q == 0, mid, lax.rem(q + 1, n_col))
    sends_on = jnp.logical_or(q == 0, jnp.logical_and(q >= mid, q < n_col - 1))
    sends_back = jnp.logical_and(q > 1, q <= mid)

    def fetch(c):
        at = pl.ds(pl.multiple_of(c * R, R), R)
        return pltpu.make_async_copy(a_ref.at[at], a_v.at[at], a_in.at[c])

    def hop(c):
        at = pl.ds(pl.multiple_of(c * S, S), S)
        return pltpu.make_async_remote_copy(
            src_ref=pack.at[at], dst_ref=pack.at[at], send_sem=f_send.at[c], recv_sem=f_recv.at[c],
            device_id=(p, target_q), device_id_type=MESH,
        )

    def hop_back(c):
        at = pl.ds(pl.multiple_of(c * S, S), S)
        return pltpu.make_async_remote_copy(
            src_ref=pack.at[at], dst_ref=pack.at[at], send_sem=b_send.at[c], recv_sem=f_recv.at[c],
            device_id=(p, lax.rem(q + n_col - 1, n_col)), device_id_type=MESH,
        )

    def peer(i):
        return lax.rem(p + i, n_row), q

    def send_corner(i):
        return pltpu.make_async_remote_copy(
            src_ref=pack.at[pl.ds(0, B)], dst_ref=corner_b, send_sem=k_send.at[i - 1], recv_sem=k_recv.at[0],
            device_id=peer(i), device_id_type=MESH,
        )

    def send_cols(i, slot):
        return pltpu.make_async_remote_copy(
            src_ref=pack.at[pl.ds(0, H)], dst_ref=cols_b.at[slot], send_sem=c_send.at[i - 1],
            recv_sem=c_recv.at[slot], device_id=peer(i), device_id_type=MESH,
        )

    barrier = pltpu.get_barrier_semaphore()

    @pl.when(q > 0)
    def _():
        pl.semaphore_signal(barrier, inc=1, device_id=(p, source_q), device_id_type=MESH)

    for i in range(1, n_row):
        pl.semaphore_signal(barrier, inc=1, device_id=peer(i), device_id_type=MESH)

    @pl.when(sends_on)
    def _():
        pl.semaphore_signal(barrier, inc=1, device_id=(p, target_q), device_id_type=MESH)

    @pl.when(sends_back)
    def _():
        pl.semaphore_signal(barrier, inc=1, device_id=(p, q - 1), device_id_type=MESH)

    early = min(EARLY, n)
    for c in range(early):
        fetch(c).start()

    ends = jnp.where(q > 0, 1, 0) + jnp.where(sends_on, 1, 0) + jnp.where(sends_back, 1, 0)
    pl.semaphore_wait(barrier, n_row - 1 + ends)

    lane = lax.broadcasted_iota(jnp.int32, (H, LANES), 1)

    def source(c):
        fetch(c).wait()
        base = pl.multiple_of(c * R, R)
        top = a_v[pl.ds(base, H), :LANES]
        low = a_v[pl.ds(base + H, H), :LANES]
        pack[pl.ds(pl.multiple_of(c * H, H), H), :] = jnp.where(lane < B, top, pltpu.roll(low, B, 1))
        for part in range(SPLIT):
            hop(c * SPLIT + part).start()

    def forward(h):
        @pl.when(q > 0)
        def _():
            hop(h).wait_recv()

            @pl.when(sends_on)
            def _():
                hop(h).start()

            @pl.when(sends_back)
            def _():
                hop_back(h).start()

    parts = n * SPLIT
    sent = 0

    def advance(count):
        nonlocal sent
        for _ in range(min(count, parts - sent)):
            forward(sent)
            sent += 1

    @pl.when(q == 0)
    def _():
        for c in range(early):
            source(c)

    @pl.loop(early, n)
    def _(c):
        fetch(c).start()

    advance(SPLIT)

    @pl.when(q > 0)
    def _():
        fetch(0).wait()

    head[...] = a_v[:B, :]
    mine = p // n_col
    owner = lax.rem(p, n_col) == q

    @pl.when(p == 0)
    def _():
        for i in range(1, n_row):
            send_corner(i).start()
        corner_b[...] = pack[:B, :]

    advance(2)

    @pl.when(owner)
    def _():
        for i in range(1, n_row):
            send_cols(i, mine).start()
        cols_b[mine] = pack[:H, :]

    @pl.when(q == 0)
    def _():
        @pl.loop(early, n)
        def _(c):
            source(c)

    advance(LEAD)

    @pl.when(p != 0)
    def _():
        send_corner(1).wait_recv()

    raw = corner_b[...][:, :B]
    corner = (raw + raw.T) / 2.0
    row64 = lax.broadcasted_iota(jnp.int32, (B, B), 0)
    col64 = lax.broadcasted_iota(jnp.int32, (B, B), 1)
    eye = jnp.where(row64 == col64, 1.0, 0.0)
    aug = jnp.concatenate([corner, eye], axis=1)
    blocks = [aug[i:i + 8] for i in range(0, B, 8)]
    row_id = lax.broadcasted_iota(jnp.int32, (8, 1), 0)
    for k in range(B):
        b, at = divmod(k, 8)
        row = blocks[b][at:at + 1, :]
        scaled = row / row[:, k:k + 1]
        for r in range(b, B // 8):
            weight = blocks[r][:, k:k + 1]
            if r == b:
                weight = jnp.where(row_id > at, weight, 0.0)
            blocks[r] = blocks[r] - weight * scaled
        if k % GROUP == GROUP - 1:
            advance(1)
    aug = jnp.concatenate(blocks, axis=0)
    pivots = jnp.sum(jnp.where(row64 == col64, aug[:, :B], 0.0), axis=1, keepdims=True)
    inv = pltpu.roll(aug, B, 1)[:, :B] / jnp.sqrt(pivots)
    inv_t = inv.T
    advance(1)
    sinv = mm(inv_t, inv, (1, 0))

    for slot in range(per):
        @pl.when(p != q + slot * n_col)
        def _(slot=slot):
            send_cols(1, slot).wait_recv()

    tiles = []
    for j in range(width // B):
        at = j // per * B
        block = cols_b[j % per, at % H:at % H + B, :]
        if at >= H:
            block = pltpu.roll(block, B, 1)
        tiles.append(block[:, :B])
    advance(1)
    m = mm(sinv, jnp.concatenate(tiles, axis=0), (1, 1))
    advance(1)
    first = q == 0
    m_first = jnp.where(first, -inv_t, m[:, :B])
    m = jnp.concatenate([m_first, m[:, B:]], axis=1)
    m_hi = m.astype(jnp.bfloat16)
    m_lo = (m - m_hi.astype(jnp.float32)).astype(jnp.bfloat16)
    m_b[...] = jnp.zeros_like(m_b)
    for i, term in enumerate((m_hi, m_hi, m_lo)):
        m_b[i * LANES:i * LANES + B, :width] = term
        m_b[i * LANES + B:(i + 1) * LANES, width:] = term
    advance(1)
    factor = jnp.where(row64 >= col64, mm(corner, inv_t, (1, 0)), 0.0)
    head[:, :B] = jnp.where(first, factor, head[:, :B])
    wide = lax.broadcasted_iota(jnp.int32, (H, width), 1)
    drop = jnp.logical_and(first, wide < B)

    def update(c):
        @pl.when(jnp.logical_and(q > 0, c > 0))
        def _():
            fetch(c).wait()

        @pl.when(c < n - TAIL)
        def _():
            apply(c)

    def apply(c):
        change = product(pack[pl.ds(pl.multiple_of(c * H, H), H), :], m_b)
        base = pl.multiple_of(c * R, R)
        for half in range(2):
            at = pl.ds(base + half * H, H)
            a_v[at, :] = jnp.where(drop, 0.0, a_v[at, :]) - change[:, half * width:(half + 1) * width]

        @pl.when(jnp.logical_and(p == 0, c == 0))
        def _():
            a_v[:B, :] = head[...]

    step = SPLIT // 2
    behind = min(sent // step, (parts - sent) // step)
    caught = behind * step == sent

    @pl.loop(0, behind)
    def _(c):
        for part in range(step):
            forward(sent + c * step + part)
        update(c)

    @pl.loop(behind, n)
    def _(c):
        if caught:
            for part in range(SPLIT):
                forward(c * SPLIT + part)
        update(c)

    @pl.when(sends_on)
    def _():
        @pl.loop(0, n * SPLIT)
        def _(c):
            hop(c).wait_send()

    @pl.when(sends_back)
    def _():
        @pl.loop(0, n * SPLIT)
        def _(c):
            hop_back(c).wait_send()

    @pl.when(p == 0)
    def _():
        for i in range(1, n_row):
            send_corner(i).wait_send()

    @pl.when(owner)
    def _():
        for i in range(1, n_row):
            send_cols(i, mine).wait_send()


def write_out(x_ref, pack, m_ref, o_ref, tail, sems):
    rows, width = x_ref.shape
    body = rows // R - TAIL
    step = body * R
    copies = [pltpu.make_async_copy(x_ref.at[pl.ds(0, step)], o_ref.at[pl.ds(0, step)], sems.at[0])]
    copies[0].start()
    first = lax.axis_index("col") == 0
    drop = jnp.logical_and(first, lax.broadcasted_iota(jnp.int32, (H, width), 1) < B)
    for i in range(TAIL):
        c = body + i
        change = product(pack[c * H:(c + 1) * H, :], m_ref)
        for half in range(2):
            old = jnp.where(drop, 0.0, x_ref[c * R + half * H:c * R + (half + 1) * H, :])
            tail[i * R + half * H:i * R + (half + 1) * H, :] = old - change[:, half * width:(half + 1) * width]
        copies.append(pltpu.make_async_copy(
            tail.at[pl.ds(i * R, R)], o_ref.at[pl.ds(c * R, R)], sems.at[1 + i]))
        copies[-1].start()
    for copy in copies:
        copy.wait()


def solution(mesh):
    n_row, n_col = mesh.shape["row"], mesh.shape["col"]

    def step(matrix):
        rows, width = matrix.shape
        n = rows // R
        per = n_row // n_col
        assert rows % R == 0 and n_row % n_col == 0 and width // B // per * B <= R
        updated = pl.pallas_call(
            functools.partial(kernel, n_row, n_col),
            out_shape=[
                jax.ShapeDtypeStruct((rows, width), jnp.float32),
                jax.ShapeDtypeStruct((rows // 2, LANES), jnp.float32),
                jax.ShapeDtypeStruct((3 * LANES, 2 * width), jnp.bfloat16),
            ],
            in_specs=[pl.BlockSpec(memory_space=pltpu.HBM)],
            out_specs=[pl.BlockSpec(memory_space=pltpu.VMEM)] * 3,
            scratch_shapes=[
                pltpu.VMEM((B, LANES), jnp.float32),
                pltpu.VMEM((per, H, LANES), jnp.float32),
                pltpu.VMEM((B, width), jnp.float32),
                pltpu.SemaphoreType.DMA((n,)),
                pltpu.SemaphoreType.DMA((n * SPLIT,)),
                pltpu.SemaphoreType.DMA((n * SPLIT,)),
                pltpu.SemaphoreType.DMA((n * SPLIT,)),
                pltpu.SemaphoreType.DMA((n_row - 1,)),
                pltpu.SemaphoreType.DMA((1,)),
                pltpu.SemaphoreType.DMA((n_row - 1,)),
                pltpu.SemaphoreType.DMA((per,)),
            ],
            compiler_params=pltpu.CompilerParams(
                collective_id=0, has_side_effects=True, vmem_limit_bytes=24 * 1024 * 1024
            ),
        )(pltpu.with_memory_space_constraint(matrix, pltpu.HBM))
        return pl.pallas_call(
            write_out,
            out_shape=pltpu.HBM((rows, width), jnp.float32),
            in_specs=[pl.BlockSpec(memory_space=pltpu.VMEM)] * 3,
            out_specs=pl.BlockSpec(memory_space=pltpu.HBM),
            scratch_shapes=[pltpu.VMEM((TAIL * R, width), jnp.float32), pltpu.SemaphoreType.DMA((1 + TAIL,))],
            compiler_params=pltpu.CompilerParams(vmem_limit_bytes=24 * 1024 * 1024),
        )(*[pltpu.with_memory_space_constraint(x, pltpu.VMEM) for x in updated])

    return jax.shard_map(
        step, mesh=mesh, in_specs=(P("row", "col"),), out_specs=P("row", "col"), check_vma=False
    )
```
